128 devices in a mesh: seq: 32 (over z, y, core), head: 4 (over x).
Axes of the slice: x: 4, y: 4, z: 4, core: 2. Of those that a mesh axis runs over, the one named last changes fastest.
Arguments:
- tokens: bfloat16 [8192, 2048], P('seq'), may hold values from -6 to 6
- turn_ids: int32 [8192], P('seq'), may hold values from 1 to 8, as said below
- q_weight: bfloat16 [2048, 2048], P(None, 'head'), may hold values from -0.125 to 0.125
- k_weight: bfloat16 [2048, 4096], P(None, 'head'), may hold values from -0.125 to 0.125
- v_weight: bfloat16 [2048, 4096], P(None, 'head'), may hold values from -0.125 to 0.125
- beta_weight: bfloat16 [2048, 32], P(None, 'head'), may hold values from -0.0625 to 0.0625
- beta_bias: float32 [32], P('head'), may hold values from -6 to 6
- norm_gain: float32 [2048], P('head'), may hold values from 0.1 to 1.9
- out_weight: bfloat16 [2048, 2048], P('head'), may hold values from -0.125 to 0.125
Outputs:
- mixed: bfloat16 [8192, 2048], P(('seq', 'head'))
The draws below stay inside these ranges and needn't reach their ends.
Inputs may be any that keep to these rules, and one draw needn't show every extreme that they name: `turn_ids`: turn numbers never fall along the sequence; every turn holds 1 to 2048 tokens and one holds exactly 2048.
All inputs are finite; a program needn't handle non-finite values.
Results may differ from the reference program's by a relative error of at most 0.018.
Values may be sent and summed in bfloat16 or wider, within the bound.
A program may use at most 128 MiB of HBM per device.

```python
import jax
import jax.numpy as jnp
from jax import lax

D = 2048
HEADS = 16
DK = 128
DV = 128
SPAN = 64
TURNS = 8
TOKENS = 8192
MOST_TURN = 2048
N_HEAD = 4


def draw_turn_ids(key, part):
    key = jax.random.fold_in(key, 11)
    subkeys = jax.random.split(key, 6)
    longest = MOST_TURN
    quarter = SPAN // 4
    block_index = jax.random.randint(subkeys[0], (), 2 * longest // SPAN, 3 * longest // SPAN - 1)
    offset = jax.random.randint(subkeys[1], (), 1, quarter + 1)
    shorts = jax.random.randint(subkeys[2], (3,), 1, quarter + 1)
    cluster_start = (block_index * SPAN + offset).astype(jnp.int32)
    short_ends = (cluster_start + jnp.cumsum(shorts)).astype(jnp.int32)
    finish = short_ends[2]
    first_cut = jax.random.randint(subkeys[3], (), cluster_start - longest, 2 * longest + 1)
    last_cut = jax.random.randint(subkeys[4], (), 3 * longest, finish + longest + 1)
    bounds = jnp.stack([jnp.array(longest, jnp.int32), first_cut.astype(jnp.int32), cluster_start, short_ends[0], short_ends[1], finish, last_cut.astype(jnp.int32)])
    position = jnp.arange(TOKENS, dtype=jnp.int32)
    turn_numbers = jnp.sum((position[:, None] >= bounds[None, :]).astype(jnp.int32), axis=1).astype(jnp.int32)
    mirrored = (TURNS - 1 - turn_numbers[::-1]).astype(jnp.int32)
    mirror_flag = jax.random.randint(subkeys[5], (), 0, 2)
    return (jnp.where(mirror_flag == 1, mirrored, turn_numbers) + 1).astype(jnp.int32)


def shard_levels(stream_key, shape, cuts, least, top_value):
    level, own = 1.0, jax.random.fold_in(stream_key, 6)
    for axis_at, blocks in cuts:
        draws = jnp.exp(jax.random.uniform(jax.random.fold_in(own, axis_at), (blocks,), jnp.float32, least / len(cuts), top_value / len(cuts)))
        level = level * jnp.repeat(draws, shape[axis_at] // blocks).reshape([-1 if axis == axis_at else 1 for axis in range(len(shape))])
    return level


def centred(key, dims, deviation, most, cuts=(), kind=jnp.bfloat16):
    values = deviation * jax.random.normal(key, dims, jnp.float32)
    if cuts:
        values = values * shard_levels(key, dims, cuts, -0.22, 0.18)
    return jnp.clip(values, -most, most).astype(kind)


def setup_inputs(seed: int = 0) -> dict:
    streams_of = jax.random.split(jax.random.key(seed), 10)
    tokens = centred(streams_of[0], (TOKENS, D), 1.0, 6.0, ((0, 32),))
    turn_ids = draw_turn_ids(jax.random.fold_in(streams_of[9], 71), 0)
    q_weight = centred(streams_of[2], (D, HEADS * DK), D ** -0.5, 0.125, ((1, 4),))
    k_weight = centred(streams_of[3], (D, HEADS * 2 * DK), D ** -0.5, 0.125, ((1, 4),))
    v_weight = centred(streams_of[4], (D, HEADS * 2 * DV), D ** -0.5, 0.125, ((1, 4),))
    beta_weight = centred(streams_of[5], (D, HEADS * 2), (4 * D) ** -0.5, 0.0625, ((1, 4),))
    beta_bias = jnp.clip(jax.random.uniform(streams_of[6], (HEADS * 2,), jnp.float32, -6.0, 6.0) * shard_levels(streams_of[6], (HEADS * 2,), ((0, 4),), -0.4, 0.0), -6.0, 6.0)
    norm_gain = jnp.clip(1.0 + 0.18 * jax.random.normal(streams_of[7], (HEADS * DV,), jnp.float32), 0.1, 1.9)
    out_weight = centred(streams_of[8], (HEADS * DV, D), (HEADS * DV) ** -0.5, 0.125, ((0, 4),))
    return dict(tokens=tokens, turn_ids=turn_ids, q_weight=q_weight, k_weight=k_weight, v_weight=v_weight, beta_weight=beta_weight, beta_bias=beta_bias, norm_gain=norm_gain, out_weight=out_weight)


key_eps = 1e-06
norm_eps = 1e-05

def normalize(vectors):
    return vectors * lax.rsqrt(lax.optimization_barrier(jnp.sum(vectors * vectors, axis=-1, keepdims=True)) + key_eps)

def project(tokens, q_weight, k_weight, v_weight, beta_weight, beta_bias):
    rows = tokens.shape[0]
    queries = jnp.dot(tokens.astype(jnp.float32), q_weight.astype(jnp.float32), preferred_element_type=jnp.float32).reshape(rows, -1, DK)
    keys = jnp.dot(tokens.astype(jnp.float32), k_weight.astype(jnp.float32), preferred_element_type=jnp.float32).reshape(rows, -1, 2, DK)
    values = jnp.dot(tokens.astype(jnp.float32), v_weight.astype(jnp.float32), preferred_element_type=jnp.float32).reshape(rows, -1, 2, DV)
    logits = jnp.dot(tokens.astype(jnp.float32), beta_weight.astype(jnp.float32), preferred_element_type=jnp.float32) + beta_bias
    betas = (2.0 * jax.nn.sigmoid(logits)).reshape(rows, -1, 2)
    return (normalize(queries), normalize(keys), values, betas)

def blocks(queries, keys, values, betas, turn_ids):
    rows, heads = (queries.shape[0], queries.shape[1])
    count = rows // SPAN
    query_blocks = queries.transpose(1, 0, 2).reshape(heads, count, SPAN, DK)
    key_blocks = keys.transpose(1, 0, 2, 3).reshape(heads, count, 2 * SPAN, DK)
    value_blocks = values.transpose(1, 0, 2, 3).reshape(heads, count, 2 * SPAN, DV)
    beta_blocks = betas.transpose(1, 0, 2).reshape(heads, count, 2 * SPAN)
    turn_blocks = turn_ids.reshape(count, SPAN)
    return (query_blocks, key_blocks, value_blocks, beta_blocks, turn_blocks)

def span_terms(queries, keys, values, betas, turns, before):
    highest = lax.Precision.HIGHEST
    refl_count = keys.shape[0]
    tok_count = queries.shape[0]
    turn_refl = jnp.repeat(turns, 2)
    carried = (turn_refl == before).astype(jnp.float32)
    same_turn = turn_refl[:, None] == turn_refl[None, :]
    key_gram = jnp.dot(keys, keys.T, precision=highest)
    lower = jnp.tril(jnp.where(same_turn, key_gram, 0.0), -1)
    system = jnp.eye(refl_count, dtype=jnp.float32) + betas[:, None] * lower
    solved = jax.scipy.linalg.solve_triangular(system, jnp.diag(betas), lower=True)
    solved_keys = jnp.dot(solved, carried[:, None] * keys, precision=highest)
    solved_values = jnp.dot(solved, values, precision=highest)
    last_turn = (turn_refl == turn_refl[-1]).astype(jnp.float32)
    lift = carried[-1] * jnp.eye(DK, dtype=jnp.float32) - jnp.dot(keys.T, last_turn[:, None] * solved_keys, precision=highest)
    write = jnp.dot(keys.T, last_turn[:, None] * solved_values, precision=highest)
    scores = jnp.dot(queries, keys.T, precision=highest)
    visible = (jnp.arange(refl_count)[None, :] // 2 <= jnp.arange(tok_count)[:, None]) & (turns[:, None] == turn_refl[None, :])
    masked = jnp.where(visible, scores, 0.0)
    local_out = jnp.dot(masked, solved_values, precision=highest)
    query_live = (turns == before).astype(jnp.float32)
    through = query_live[:, None] * queries - jnp.dot(masked, solved_keys, precision=highest)
    return (lift, write, local_out, through)

def finish(outputs, norm_gain):
    scaled = outputs * lax.rsqrt(lax.optimization_barrier(jnp.mean(outputs * outputs, axis=-1, keepdims=True)) + norm_eps)
    return (scaled.reshape(outputs.shape[0], -1) * norm_gain).astype(jnp.bfloat16)

def reference(tokens, turn_ids, q_weight, k_weight, v_weight, beta_weight, beta_bias, norm_gain, out_weight):
    highest = lax.Precision.HIGHEST
    queries, keys, values, betas = project(tokens, q_weight, k_weight, v_weight, beta_weight, beta_bias)
    before = jnp.concatenate([jnp.full((1,), -1, jnp.int32), turn_ids[:-1].astype(jnp.int32)])[::SPAN]
    query_blocks, key_blocks, value_blocks, beta_blocks, turn_blocks = blocks(queries, keys, values, betas, turn_ids)

    def per_head(operands):
        query_head, key_head, value_head, beta_head = operands
        lift, write, local_out, through = jax.vmap(span_terms)(query_head, key_head, value_head, beta_head, turn_blocks, before)

        def advance(state, items):
            lift_block, write_block, local_block, through_block = items
            result = local_block + jnp.dot(through_block, state, precision=highest)
            return (jnp.dot(lift_block, state, precision=highest) + write_block, result)
        final, results = lax.scan(advance, jnp.zeros((DK, DV), jnp.float32), (lift, write, local_out, through))
        return results
    results = lax.map(per_head, (query_blocks, key_blocks, value_blocks, beta_blocks))
    outputs = results.transpose(1, 2, 0, 3).reshape(TOKENS, HEADS, DV)
    hidden = finish(outputs, norm_gain)
    width = HEADS * DV // N_HEAD
    total = jnp.zeros((TOKENS, D), jnp.float32)
    for group in range(N_HEAD):
        partial_sum = jnp.dot(hidden[:, group * width:(group + 1) * width].astype(jnp.float32), out_weight[group * width:(group + 1) * width].astype(jnp.float32), preferred_element_type=jnp.float32).astype(jnp.bfloat16)
        total = total + lax.optimization_barrier(partial_sum).astype(jnp.float32)
    return total.astype(jnp.bfloat16)
```

```python
import functools

import jax
import jax.numpy as jnp
from jax import lax
from jax.experimental import pallas as pl
from jax.experimental.pallas import tpu as pltpu
from jax.sharding import PartitionSpec as P

F32, BF16 = jnp.float32, jnp.bfloat16
MESH = pl.DeviceIdType.MESH
DK = 128
BLK = 128
REFL = 2 * BLK
NB = 4
HERE = 2
key_eps = 1e-06
norm_eps = 1e-05

NN = (((1,), (0,)), ((), ()))
NT = (((1,), (1,)), ((), ()))


def dot(a, b, dims=NN):
    return lax.dot_general(a, b, dims, preferred_element_type=F32)


def halves(a):
    hi = a.astype(BF16)
    return hi, (a - hi.astype(F32)).astype(BF16)


def mm1(a, b, dims=NN):
    return dot(a.astype(BF16), b.astype(BF16), dims)


def mm3(a, b, dims=NN):
    ah, al = halves(a)
    bh, bl = halves(b)
    return dot(ah, bh, dims) + (dot(ah, bl, dims) + dot(al, bh, dims))


def iota(shape, axis):
    return lax.broadcasted_iota(jnp.int32, shape, axis)


def interleave(a, b):
    rows = a.shape[0]
    a = a.reshape(rows // 8, 1, 8, a.shape[1])
    b = b.reshape(rows // 8, 1, 8, b.shape[3] if b.ndim == 4 else b.shape[1])
    return jnp.concatenate([a, b], axis=1).reshape(2 * rows, a.shape[3])


def token_of(r):
    return (r // 16) * 8 + r % 8


def time_of(r):
    return token_of(r) * 2 + (r // 8) % 2


def normalize(v):
    return v * lax.rsqrt(jnp.sum(v * v, axis=-1, keepdims=True) + key_eps)


def kernel(
    tok, ids, qw, kw, vw, bw, bb, gain, ow,
    out,
    x_s, wk_s, wv_s, wq_s, bw_s, wo_s, ids_s, prev_s,
    k_s, v_s, q_s, beta_s, mask_s, vis_s, tid_s, edge_s, spread_s,
    cs_s, bc_s, xs_s, u_s, kt_s, pre_s, thr_s,
    send_s, recv_s, wrecv_s, hid_s, hid2_s, rs_s, rr_s,
    lsem, tsem, isem, esend, erecv, hsem, rsend, rrecv,
):
    seq = lax.axis_index("seq")
    head = lax.axis_index("head")
    nseq = lax.axis_size("seq")
    nhead = lax.axis_size("head")
    chips = nseq // 2
    chip, core = seq // 2, lax.rem(seq, 2)
    other = 1 - core

    def at(step, which):
        return (lax.rem(chip + step + chips, chips) * 2 + which, head)

    def along(step):
        return (seq, lax.rem(head + step + nhead, nhead))

    own_rows = pl.ds(pl.multiple_of(core * 256, 256), 256)
    col = lambda size, at_: pl.ds(pl.multiple_of(core * (2 * size) + at_, 128), size)
    local = [
        pltpu.make_async_copy(tok, x_s.at[own_rows], lsem.at[0]),
        pltpu.make_async_copy(ids, ids_s.at[core], lsem.at[1]),
        pltpu.make_async_copy(kw.at[:, pl.ds(pl.multiple_of(core * 512, 256), 256)], wk_s.at[0], lsem.at[2]),
        pltpu.make_async_copy(kw.at[:, pl.ds(pl.multiple_of(core * 512 + 256, 256), 256)], wk_s.at[1], lsem.at[3]),
        pltpu.make_async_copy(bw, bw_s, lsem.at[4]),
        pltpu.make_async_copy(vw.at[:, pl.ds(pl.multiple_of(core * 512, 256), 256)], wv_s.at[0], lsem.at[5]),
        pltpu.make_async_copy(vw.at[:, pl.ds(pl.multiple_of(core * 512 + 256, 256), 256)], wv_s.at[1], lsem.at[6]),
        pltpu.make_async_copy(qw.at[:, pl.ds(pl.multiple_of(core * 256, 256), 256)], wq_s, lsem.at[7]),
        pltpu.make_async_copy(ow, wo_s, lsem.at[8]),
    ]
    for c in local:
        c.start()

    barrier = pltpu.get_barrier_semaphore()
    peers = [at(0, other)]
    for step in (1, 2, 3, 4, -1, -2, -3, -4):
        peers.append(at(step, core))
    for step in (1, -1):
        peers.append(at(step, other))
        peers.append(along(step))
    for peer in peers:
        pl.semaphore_signal(barrier, inc=1, device_id=peer, device_id_type=MESH)
    pl.semaphore_wait(barrier, len(peers))

    def remote(src, dst, ssem, rsem, peer):
        return pltpu.make_async_remote_copy(
            src_ref=src, dst_ref=dst, send_sem=ssem, recv_sem=rsem, device_id=peer, device_id_type=MESH
        )

    swap_ids = remote(ids, ids_s.at[core], isem.at[0], isem.at[1], at(0, other))
    swap_ids.start()
    swap_tok = remote(tok, x_s.at[own_rows], tsem.at[0], tsem.at[1], at(0, other))
    swap_tok.start()
    next_same = remote(ids, prev_s.at[core], isem.at[2], isem.at[3], at(1, core))
    next_same.start()
    next_other = remote(ids, prev_s.at[core], isem.at[4], isem.at[5], at(1, other))
    next_other.start()

    sr, sc = iota((128, 2048), 0), iota((128, 2048), 1)
    spread_s[...] = ((sr // 16 == (sc % 128) // 16) & (sr % 16 == sc // 128)).astype(F32).astype(BF16)

    def project(rows):
        x = x_s[rows, :]
        for h in range(HERE):
            k_s[h, rows, :] = dot(x, wk_s[h])
        for h in range(HERE):
            v_s[h, rows, :] = dot(x, wv_s[h])
        q_s[rows, :] = dot(x, wq_s[...])
        logits = dot(x, bw_s[...]) + bb[...]
        beta_s[rows, :] = 2.0 * jax.nn.sigmoid(logits)

    for c in local[:8]:
        c.wait()
    project(own_rows)
    swap_tok.wait()
    project(pl.ds(pl.multiple_of(other * 256, 256), 256))

    swap_ids.wait()
    next_same.wait()
    next_other.wait()
    rr_, cc_ = iota((REFL, REFL), 0), iota((REFL, REFL), 1)
    earlier = time_of(rr_) > time_of(cc_)
    seen = token_of(iota((BLK, REFL), 1)) <= iota((BLK, REFL), 0)
    for b in range(NB):
        row = ids_s[b // 2, pl.ds(b % 2, 1), :].astype(F32)
        if b == 0:
            before = jnp.max(prev_s[1, pl.ds(1, 1), :].astype(F32), axis=1, keepdims=True)
            before = jnp.where(chip == 0, -1.0, before)
        else:
            before = jnp.max(ids_s[(b - 1) // 2, pl.ds((b - 1) % 2, 1), :].astype(F32), axis=1, keepdims=True)
        last = jnp.max(row, axis=1, keepdims=True)
        tcol = jnp.transpose(jnp.broadcast_to(row, (BLK, BLK)))
        rcol = interleave(tcol, tcol)
        rrow = jnp.transpose(rcol)
        mask_s[b] = jnp.where(
            earlier & (jnp.concatenate([rcol, rcol], axis=1) == jnp.concatenate([rrow, rrow], axis=0)), 1.0, 0.0
        )
        vis_s[b] = jnp.where(seen & (jnp.concatenate([tcol, tcol], axis=1) == rrow), 1.0, 0.0)
        tid_s[b] = tcol
        edge_s[b, 0] = jnp.broadcast_to(before, (BLK, 128))
        edge_s[b, 1] = jnp.broadcast_to(last, (BLK, 128))

    r128, c128 = iota((128, 128), 0), iota((128, 128), 1)
    eye = (r128 == c128).astype(F32)

    def level(t, a, size):
        odd = jnp.where(((r128 // (2 * size)) == (c128 // (2 * size))) & ((r128 // size) % 2 == 1) & ((c128 // size) % 2 == 0), a, 0.0)
        pick = lambda m: jnp.concatenate([m[i * size:(i + 1) * size] for i in range(1, 128 // size, 2)], axis=0)
        low = mm3(pick(odd), t)
        zero = jnp.zeros((size, 128), F32)
        full = jnp.concatenate(
            [piece for i in range(64 // size) for piece in (zero, low[i * size:(i + 1) * size])], axis=0
        )
        new = pick(t) - mm3(pick(t), full)
        return jnp.concatenate(
            [piece for i in range(64 // size) for piece in (t[2 * i * size:(2 * i + 1) * size], new[i * size:(i + 1) * size])],
            axis=0,
        )

    def maps(h, carry):
        betas = beta_s[...]
        lane = iota(betas.shape, 1)
        b0 = jnp.sum(jnp.where(lane == core * 4 + h * 2, betas, 0.0), axis=1, keepdims=True)
        b1 = jnp.sum(jnp.where(lane == core * 4 + h * 2 + 1, betas, 0.0), axis=1, keepdims=True)
        systems, rhs, kts = [], [], []
        for b in range(NB):
            rows = pl.ds(b * BLK, BLK)
            k0 = normalize(k_s[h, rows, 0:128])
            k1 = normalize(k_s[h, rows, 128:256])
            v0 = v_s[h, rows, 0:128]
            v1 = v_s[h, rows, 128:256]
            c0, c1 = b0[b * BLK:(b + 1) * BLK], b1[b * BLK:(b + 1) * BLK]
            keys = interleave(k0, k1)
            bkeys = interleave(c0 * k0, c1 * k1)
            bvals = interleave(c0 * v0, c1 * v1)
            kt = jnp.transpose(keys)
            a = mm3(bkeys, kt) * mask_s[b]
            tcol = tid_s[b]
            live = jnp.where(tcol == edge_s[b, 0], 1.0, 0.0)
            rhs.append(jnp.concatenate([-(interleave(live, live) * bkeys), bvals], axis=1))
            kt_s[h, b] = kt
            kts.append(kt)
            systems.append(a)
            for half in range(2):
                lo = half * 128
                acc = jnp.zeros((16, 128), F32)
                lanes = iota((16, 128), 1) // 16
                for g in range(8):
                    acc = acc + jnp.where(lanes == g, a[lo + g * 16:lo + (g + 1) * 16, lo:lo + 128], 0.0)
                cs_s[:, 2 * b + half, :] = acc
        flat = cs_s[...].reshape(128, 128)
        hi, low = halves(flat)
        bc_s[...] = dot(hi, spread_s[...]) + dot(low, spread_s[...])
        solved = {}
        order = [j * 8 + t for t in range(8) for j in range(2)]
        unit = iota((8, 128), 1) % 16
        for place, i in enumerate(order):
            x = jnp.where(unit == i, 1.0, 0.0)
            for j in order[:place]:
                x = x - bc_s[i * 8:(i + 1) * 8, j * 128:(j + 1) * 128] * solved[j]
            solved[i] = x
            xs_s[i] = x
        for b in range(NB):
            a = systems[b]
            ts = []
            for half in range(2):
                lo = half * 128
                x = xs_s[:, 2 * b + half, :]
                t = jnp.where(r128 // 16 == c128 // 16, jnp.concatenate([x] * 8, axis=0), 0.0)
                for size in (16, 32, 64):
                    t = level(t, a[lo:lo + 128, lo:lo + 128], size)
                ts.append(t)
            u1 = mm3(ts[0], rhs[b][:128])
            u2 = mm3(ts[1], rhs[b][128:] - mm3(a[128:, :128], u1))
            u = jnp.concatenate([u1, u2], axis=0)
            u_s[h, b] = u
            tcol = tid_s[b]
            ending = jnp.where(tcol == edge_s[b, 1], 1.0, 0.0)
            ending = interleave(ending, ending)
            lw = mm3(kts[b], jnp.concatenate([ending, ending], axis=1) * u)
            through = jnp.where(edge_s[b, 0] == edge_s[b, 1], eye, 0.0)
            lift = lw[:, :128] + through
            write = lw[:, 128:]
            if b == 0:
                pair = jnp.concatenate([lift, write], axis=1)
            else:
                pair = mm3(lift, pair)
                pair = jnp.concatenate([pair[:, :128], pair[:, 128:] + write], axis=1)
            if b < NB - 1:
                pre_s[h, b] = pair
        send_s[h] = pair.astype(BF16)
        return carry

    def exchange(h):
        copies = [
            remote(send_s.at[h], recv_s.at[step - 1, h], esend.at[step - 1, h], erecv.at[step - 1, h], at(step, core))
            for step in (1, 2, 3)
        ]
        copies.append(
            remote(send_s.at[h, :, pl.ds(128, 128)], wrecv_s.at[h], esend.at[3, h], erecv.at[3, h], at(4, core))
        )
        return copies

    def maps_and_send(h, carry):
        maps(h, carry)
        for c in exchange(h):
            c.start()
        return carry

    lax.fori_loop(0, HERE, maps_and_send, 0)

    def local_out(h, carry):
        for b in range(NB):
            rows = pl.ds(b * BLK, BLK)
            q = normalize(q_s[rows, pl.ds(pl.multiple_of(h * 128, 128), 128)])
            scores = mm3(q, kt_s[h, b]) * vis_s[b]
            res = mm3(scores, u_s[h, b])
            live = jnp.where(tid_s[b] == edge_s[b, 0], q, 0.0)
            thr, loc = res[:, :128] + live, res[:, 128:]
            if b > 0:
                res = mm3(thr, pre_s[h, b - 1])
                thr, loc = res[:, :128], res[:, 128:] + loc
            thr_s[h, rows, :] = jnp.concatenate([thr, loc], axis=1)
        return carry

    lax.fori_loop(0, HERE, local_out, 0)
    local[8].wait()

    for h in range(HERE):
        for c in exchange(h):
            c.wait()
        state = wrecv_s[h].astype(F32)
        for step in (3, 2, 1):
            state = mm3(recv_s[step - 1, h, :, 0:128].astype(F32), state) + recv_s[step - 1, h, :, 128:256].astype(F32)
        for part in range(2):
            rows = pl.ds(part * 256, 256)
            o = thr_s[h, rows, 128:256] + mm3(thr_s[h, rows, 0:128], state)
            o = o * lax.rsqrt(jnp.mean(o * o, axis=-1, keepdims=True) + norm_eps)
            g = gain[:, pl.ds(pl.multiple_of(core * 256 + h * 128, 128), 128)]
            hid_s[part, :, h * 128:(h + 1) * 128] = (o * g).astype(BF16)

    swap_hid = remote(hid_s.at[other], hid2_s.at[core], hsem.at[0], hsem.at[1], at(0, other))
    swap_hid.start()
    hid2_s[core] = hid_s[core]
    swap_hid.wait()

    def term(step):
        rows = pl.ds(pl.multiple_of(lax.rem(head + step + nhead, nhead) * 64, 64), 64)
        return lambda cols: (
            dot(hid2_s[0, rows, :], wo_s[0:256, cols]) + dot(hid2_s[1, rows, :], wo_s[256:512, cols])
        ).astype(BF16)

    A, B = slice(0, 1024), slice(1024, 2048)
    part = (A, B)
    def hop(direction, stage):
        return remote(
            rs_s.at[direction, stage], rr_s.at[direction, stage], rsend.at[direction, stage], rrecv.at[direction, stage],
            along(1 if direction == 0 else -1),
        )

    far = term(2)
    for d in range(2):
        rs_s[d, 0] = far(part[d])
        hop(d, 0).start()
    near = (term(1), term(-1))
    for d in range(2):
        rs_s[d, 1] = near[d](part[1 - d])
        hop(d, 1).start()
    for d in range(2):
        mine = near[d](part[d]).astype(F32)
        hop(d, 0).wait()
        rs_s[d, 2] = (mine + rr_s[d, 0].astype(F32)).astype(BF16)
        hop(d, 2).start()
    own = term(0)
    sums = [own(p).astype(F32) for p in part]
    for d in range(2):
        hop(d, 1).wait()
        sums[1 - d] = sums[1 - d] + rr_s[d, 1].astype(F32)
    for d in range(2):
        hop(d, 2).wait()
        sums[d] = sums[d] + rr_s[d, 2].astype(F32)
    out[:, A] = sums[0].astype(BF16)
    out[:, B] = sums[1].astype(BF16)


def body(tokens, turn_ids, q_weight, k_weight, v_weight, beta_weight, beta_bias, norm_gain, out_weight):
    any_ = pl.BlockSpec(memory_space=pl.ANY)
    vmem = pl.BlockSpec(memory_space=pltpu.VMEM)
    V = pltpu.VMEM
    D = tokens.shape[1]
    return pl.pallas_call(
        kernel,
        out_shape=jax.ShapeDtypeStruct((64, 2048), BF16),
        in_specs=[any_] * 6 + [vmem, vmem, any_],
        out_specs=vmem,
        scratch_shapes=[
            V((512, D), BF16), V((2, D, 256), BF16), V((2, D, 256), BF16), V((D, 256), BF16), V((D, 8), BF16),
            V((512, D), BF16), V((2, 2, 128), jnp.int32), V((2, 2, 128), jnp.int32),
            V((2, 512, 256), F32), V((2, 512, 256), F32), V((512, 256), F32), V((512, 8), F32),
            V((NB, 256, 256), F32), V((NB, 128, 256), F32), V((NB, 128, 128), F32), V((NB, 2, 128, 128), F32),
            V((128, 2048), BF16),
            V((16, 8, 128), F32), V((128, 2048), F32), V((16, 8, 128), F32),
            V((2, NB, 256, 256), F32), V((2, NB, 128, 256), F32), V((2, NB - 1, 128, 256), F32), V((2, 512, 256), F32),
            V((2, 128, 256), BF16), V((3, 2, 128, 256), BF16), V((2, 128, 128), BF16),
            V((2, 256, 256), BF16), V((2, 256, 256), BF16),
            V((2, 3, 64, 1024), BF16), V((2, 3, 64, 1024), BF16),
            pltpu.SemaphoreType.DMA((9,)), pltpu.SemaphoreType.DMA((2,)), pltpu.SemaphoreType.DMA((6,)),
            pltpu.SemaphoreType.DMA((4, 2)), pltpu.SemaphoreType.DMA((4, 2)), pltpu.SemaphoreType.DMA((2,)),
            pltpu.SemaphoreType.DMA((2, 3)), pltpu.SemaphoreType.DMA((2, 3)),
        ],
        compiler_params=pltpu.CompilerParams(
            collective_id=0, has_side_effects=True, vmem_limit_bytes=56 * 1024 * 1024
        ),
        cost_estimate=pl.CostEstimate(flops=5_000_000_000, bytes_accessed=14_000_000, transcendentals=10_000),
    )(
        tokens, turn_ids.reshape(2, 128), q_weight, k_weight, v_weight, beta_weight,
        beta_bias.reshape(1, 8), norm_gain.reshape(1, 512), out_weight,
    )


def solution(mesh):
    return jax.shard_map(
        body,
        mesh=mesh,
        in_specs=(
            P("seq", None),
            P("seq"),
            P(None, "head"),
            P(None, "head"),
            P(None, "head"),
            P(None, "head"),
            P("head"),
            P("head"),
            P("head", None),
        ),
        out_specs=P(("seq", "head"), None),
        check_vma=False,
    )
```

```python
import functools

import jax
import jax.numpy as jnp
from jax import lax
from jax.experimental import pallas as pl
from jax.experimental.pallas import tpu as pltpu
from jax.sharding import PartitionSpec as P

F32, BF16 = jnp.float32, jnp.bfloat16
MESH = pl.DeviceIdType.MESH
DK = 128
BLK = 128
REFL = 2 * BLK
NB = 4
HERE = 2
REACH = 4
key_eps = 1e-06
norm_eps = 1e-05

NN = (((1,), (0,)), ((), ()))
NT = (((1,), (1,)), ((), ()))


def dot(a, b, dims=NN):
    return lax.dot_general(a, b, dims, preferred_element_type=F32)


def halves(a):
    hi = a.astype(BF16)
    return hi, (a - hi.astype(F32)).astype(BF16)


def joined(a, b):
    (ah, al), (bh, bl) = a, b
    return dot(jnp.concatenate([ah, al, ah], axis=1), jnp.concatenate([bh, bh, bl], axis=0))


def mm3(a, b):
    return joined(halves(a), halves(b))


def iota(shape, axis):
    return lax.broadcasted_iota(jnp.int32, shape, axis)


def interleave(a, b):
    groups, lanes = a.shape[0] // 8, a.shape[1]
    return jnp.concatenate(
        [a.reshape(groups, 1, 8, lanes), b.reshape(groups, 1, 8, lanes)], axis=1
    ).reshape(groups * 16, lanes)


def token_of(r):
    return (r // 16) * 8 + r % 8


def time_of(r):
    return token_of(r) * 2 + (r // 8) % 2


def normalize(v):
    return v * lax.rsqrt(jnp.sum(v * v, axis=-1, keepdims=True) + key_eps)


def kernel(
    tok, ids, qw, kw, vw, bw, bb, gain, ow,
    out,
    x_s, wk_s, wv_s, wq_s, bw_s, wo_s, ids_s, prev_s,
    k_s, v_s, q_s, beta_s, tid_s, vis_s, mask_s, end_s, spread_s,
    cs_s, bc_s, xs_s, u_s, kt_s, lw_s, duo_s, thr_s,
    send_s, recv_s, wrecv_s, hid_s, hid2_s, far_s, wf_s, rs_s, rr_s,
    lsem, tsem, isem, esend, erecv, hsem, fsem, wsem, rsend, rrecv,
):
    seq = lax.axis_index("seq")
    head = lax.axis_index("head")
    nseq = lax.axis_size("seq")
    nhead = lax.axis_size("head")
    chips = nseq // 2
    chip, core = seq // 2, lax.rem(seq, 2)
    other = 1 - core

    def at(step, which):
        return (lax.rem(chip + step + chips, chips) * 2 + which, head)

    def along(step):
        return (seq, lax.rem(head + step + nhead, nhead))

    def across(step):
        return (chip * 2 + other, lax.rem(head + step + nhead, nhead))

    own_rows = pl.ds(pl.multiple_of(core * 256, 256), 256)
    def weights(ref, width, h):
        return ref.at[:, pl.ds(pl.multiple_of(core * HERE * width + h * width, 256), 256)]

    X, K0, BW, V0, K1, V1, Q, O, IDS = range(9)
    pairs = [
        (tok, x_s.at[own_rows]), (weights(kw, 256, 0), wk_s.at[0]), (bw, bw_s), (weights(vw, 256, 0), wv_s.at[0]),
        (weights(kw, 256, 1), wk_s.at[1]), (weights(vw, 256, 1), wv_s.at[1]), (weights(qw, 128, 0), wq_s), (ow, wo_s),
        (ids, ids_s.at[core]),
    ]
    local = [pltpu.make_async_copy(src, dst, lsem.at[n]) for n, (src, dst) in enumerate(pairs)]
    for c in local:
        c.start()

    barrier = pltpu.get_barrier_semaphore()
    mutual = [at(0, other), along(1), along(-1), along(2), across(2)]
    for peer in mutual:
        pl.semaphore_signal(barrier, inc=1, device_id=peer, device_id_type=MESH)
    for step in range(1, REACH + 1):
        @pl.when(chip >= step)
        def _():
            pl.semaphore_signal(barrier, inc=1, device_id=at(-step, core), device_id_type=MESH)
            if step == 1:
                pl.semaphore_signal(barrier, inc=1, device_id=at(-step, other), device_id_type=MESH)
    greeted = len(mutual) + jnp.minimum(chips - 1 - chip, REACH) + jnp.minimum(chips - 1 - chip, 1)

    def remote(src, dst, ssem, rsem, peer):
        return pltpu.make_async_remote_copy(
            src_ref=src, dst_ref=dst, send_sem=ssem, recv_sem=rsem, device_id=peer, device_id_type=MESH
        )

    swap_ids = remote(ids, ids_s.at[core], isem.at[0], isem.at[1], at(0, other))
    swap_tok = remote(tok, x_s.at[own_rows], tsem.at[0], tsem.at[1], at(0, other))
    next_same = remote(ids, prev_s.at[core], isem.at[2], isem.at[3], at(1, core))
    half_rows = pl.ds(pl.multiple_of(core * 256, 256), 256)
    far_weights = remote(ow.at[half_rows], wf_s.at[half_rows], wsem.at[0], wsem.at[1], along(2))
    pass_weights = remote(wf_s.at[half_rows], wf_s.at[half_rows], wsem.at[2], wsem.at[3], at(0, other))
    next_other = remote(ids, prev_s.at[core], isem.at[4], isem.at[5], at(1, other))

    sr, sc = iota((128, 2048), 0), iota((128, 2048), 1)
    spread_s[...] = ((sr // 16 == (sc % 128) // 16) & (sr % 16 == sc // 128)).astype(F32).astype(BF16)

    def rows_of(half):
        return pl.ds(pl.multiple_of(half * 256, 256), 256)

    def project(rows, h):
        x = x_s[rows, :]
        k_s[h, rows, :] = dot(x, wk_s[h])
        v_s[h, rows, :] = dot(x, wv_s[h])

    def strengths(rows):
        beta_s[rows, :] = 2.0 * jax.nn.sigmoid(dot(x_s[rows, :], bw_s[...], NT) + bb[...])

    r128, c128 = iota((128, 128), 0), iota((128, 128), 1)
    eye = (r128 == c128).astype(F32)
    rr_, cc_ = iota((REFL, REFL), 0), iota((REFL, REFL), 1)
    earlier = time_of(rr_) > time_of(cc_)
    seen = token_of(iota((BLK, REFL), 1)) <= iota((BLK, REFL), 0)
    lanes16 = iota((16, 128), 1) // 16
    unit8 = iota((8, 128), 1) % 16
    order = [j * 8 + t for t in range(8) for j in range(2)]

    def odd_rows(m, size):
        return jnp.concatenate([m[i * size:(i + 1) * size] for i in range(1, 128 // size, 2)], axis=0)

    def even_rows(m, size):
        return jnp.concatenate([m[i * size:(i + 1) * size] for i in range(0, 128 // size, 2)], axis=0)

    def merged(even, odd, size):
        return jnp.concatenate(
            [m[i * size:(i + 1) * size] for i in range(64 // size) for m in (even, odd)], axis=0
        )

    def turns(half):
        for j in range(2):
            row = ids_s[half, pl.ds(j, 1), :].astype(F32)
            tcol = jnp.transpose(jnp.broadcast_to(row, (BLK, BLK)))
            rcol = interleave(tcol, tcol)
            rrow = jnp.transpose(rcol)
            mask_s[half, j] = jnp.where(
                earlier & (jnp.concatenate([rcol, rcol], axis=1) == jnp.concatenate([rrow, rrow], axis=0)), 1.0, 0.0
            )
            end_s[half, j] = jnp.where(rrow[:16] == jnp.max(row, axis=1, keepdims=True), 1.0, 0.0)
            vis_s[half, j] = jnp.where(seen & (jnp.concatenate([tcol, tcol], axis=1) == rrow), 1.0, 0.0)
            tid_s[half, j] = tcol

    def maps(units):
        systems, rhs, kts = [], [], []
        for half, h, j in units:
            block = pl.ds(pl.multiple_of(half * 256 + j * BLK, BLK), BLK)
            betas = beta_s[block, :]
            lane = iota(betas.shape, 1)
            mine = [
                jnp.sum(jnp.where(lane == core * 4 + h * 2 + r, betas, 0.0), axis=1, keepdims=True) for r in range(2)
            ]
            k0 = normalize(k_s[h, block, 0:128])
            k1 = normalize(k_s[h, block, 128:256])
            keys = interleave(k0, k1)
            bkeys = interleave(mine[0] * k0, mine[1] * k1)
            bvals = interleave(mine[0] * v_s[h, block, 0:128], mine[1] * v_s[h, block, 128:256])
            kt = halves(jnp.transpose(keys))
            kt_s[half, h, j, 0] = kt[0]
            kt_s[half, h, j, 1] = kt[1]
            systems.append(joined(halves(bkeys), kt) * mask_s[half, j])
            rhs.append(jnp.concatenate([-bkeys, bvals], axis=1))
            ending = end_s[half, j][:1].astype(BF16)
            kts.append((kt[0] * ending, kt[1] * ending))
        tiles = [a[lo:lo + 128, lo:lo + 128] for a in systems for lo in (0, 128)]
        for n, a in enumerate(tiles):
            acc = jnp.where(lanes16 == 0, a[0:16], 0.0)
            for g in range(1, 8):
                acc = jnp.where(lanes16 == g, a[g * 16:(g + 1) * 16], acc)
            for slot in range(n, 8, len(tiles)):
                cs_s[:, slot, :] = acc
        hi, low = halves(cs_s[...].reshape(128, 128))
        bc_s[...] = dot(hi, spread_s[...]) + dot(low, spread_s[...])
        solved = {}
        for place, i in enumerate(order):
            x = jnp.where(unit8 == i, 1.0, 0.0)
            for j in order[:place]:
                x = x - bc_s[i * 8:(i + 1) * 8, j * 128:(j + 1) * 128] * solved[j]
            solved[i] = x
            xs_s[i] = x
        ts = [
            jnp.where(r128 // 16 == c128 // 16, jnp.concatenate([xs_s[:, n, :]] * 8, axis=0), 0.0)
            for n in range(len(tiles))
        ]
        for size in (16, 32, 64):
            ro = odd_rows(r128, size)
            pick = (ro // (2 * size) == c128[:64] // (2 * size)) & ((c128[:64] // size) % 2 == 0)
            split = [halves(t) for t in ts]
            lows = [
                joined(halves(jnp.where(pick, odd_rows(a, size), 0.0)), t) for a, t in zip(tiles, split)
            ]
            zero = jnp.zeros((64, 128), F32)
            news = [
                joined((odd_rows(t[0], size), odd_rows(t[1], size)), halves(merged(zero, low, size)))
                for t, low in zip(split, lows)
            ]
            ts = [merged(even_rows(t, size), odd_rows(t, size) - new, size) for t, new in zip(ts, news)]
        split = [halves(t) for t in ts]
        tops = [joined(split[2 * n], halves(rhs[n][:128])) for n in range(len(units))]
        mids = [
            rhs[n][128:] - joined(halves(systems[n][128:, :128]), halves(tops[n])) for n in range(len(units))
        ]
        lows = [joined(split[2 * n + 1], halves(mids[n])) for n in range(len(units))]
        lws = []
        for n, (half, h, j) in enumerate(units):
            u = halves(jnp.concatenate([tops[n], lows[n]], axis=0))
            u_s[half, h, j, 0] = u[0]
            u_s[half, h, j, 1] = u[1]
            lws.append(joined(kts[n], u))
        for n, (half, h, j) in enumerate(units):
            last = jnp.max(ids_s[half, pl.ds(j, 1), :].astype(F32), axis=1, keepdims=True)
            lift = jnp.where(before(half, j) == last, eye + lws[n][:, :128], 0.0)
            lws[n] = jnp.concatenate([lift, lws[n][:, 128:]], axis=1)
            lw_s[half, h, j] = lws[n]
        for n, (half, h, j) in enumerate(units):
            if j == 1:
                duo_s[half, h] = after(lws[n], lws[n - 1])

    def after(late, early):
        pair = mm3(late[:, :128], early)
        return jnp.concatenate([pair[:, :128], pair[:, 128:] + late[:, 128:]], axis=1)

    def before(half, j):
        if j == 1:
            return jnp.max(ids_s[half, pl.ds(0, 1), :].astype(F32), axis=1, keepdims=True)
        first = jnp.max(prev_s[1, pl.ds(1, 1), :].astype(F32), axis=1, keepdims=True)
        first = jnp.where(chip == 0, -1.0, first)
        inner = jnp.max(ids_s[0, pl.ds(1, 1), :].astype(F32), axis=1, keepdims=True)
        return jnp.where(half == 0, first, inner)

    def exchange(h, step):
        if step == REACH:
            return remote(
                send_s.at[h, :, pl.ds(128, 128)], wrecv_s.at[h], esend.at[step - 1, h], erecv.at[step - 1, h], at(step, core)
            )
        return remote(
            send_s.at[h], recv_s.at[step - 1, h], esend.at[step - 1, h], erecv.at[step - 1, h], at(step, core)
        )

    def send_maps(h):
        send_s[h] = after(duo_s[1, h], duo_s[0, h]).astype(BF16)
        for step in range(1, REACH + 1):
            @pl.when(chip + step < chips)
            def _():
                exchange(h, step).start()

    for n in (X, K0, V0):
        local[n].wait()
    project(rows_of(core), 0)
    pl.semaphore_wait(barrier, greeted)
    for c in (swap_ids, swap_tok, far_weights):
        c.start()

    @pl.when(chip + 1 < chips)
    def _():
        next_same.start()
        next_other.start()

    for step in range(1, REACH + 1):
        @pl.when(chip < step)
        def _():
            if step == REACH:
                wrecv_s[...] = jnp.zeros_like(wrecv_s)
            else:
                recv_s[step - 1] = jnp.zeros(recv_s.shape[1:], BF16)
            if step == 1:
                prev_s[...] = jnp.zeros_like(prev_s)

    for n in (BW, IDS):
        local[n].wait()
    strengths(rows_of(core))
    turns(core)
    swap_ids.wait()

    @pl.when(chip >= 1)
    def _():
        next_same.wait_recv()
        next_other.wait_recv()

    maps([(core, 0, 0), (core, 0, 1)])
    turns(other)
    swap_tok.wait()
    project(rows_of(other), 0)
    strengths(rows_of(other))
    maps([(other, 0, 0), (other, 0, 1)])
    send_maps(0)
    for n in (K1, V1):
        local[n].wait()
    project(slice(None), 1)
    maps([(0, 1, 0), (0, 1, 1), (1, 1, 0), (1, 1, 1)])
    send_maps(1)

    local[Q].wait()
    q_s[...] = dot(x_s[...], wq_s[...])

    def local_out(h, carry):
        second = duo_s[0, h]
        pre = (None, lw_s[0, h, 0], second, after(lw_s[1, h, 0], second))
        blocks = [(b // 2, b % 2) for b in range(NB)]
        qs = [
            normalize(q_s[pl.ds(b * BLK, BLK), pl.ds(pl.multiple_of(h * 128, 128), 128)]) for b in range(NB)
        ]
        scores = [
            joined(halves(qs[b]), (kt_s[p, h, j, 0], kt_s[p, h, j, 1])) * vis_s[p, j] for b, (p, j) in enumerate(blocks)
        ]
        res = [
            joined(halves(scores[b]), (u_s[p, h, j, 0], u_s[p, h, j, 1])) for b, (p, j) in enumerate(blocks)
        ]
        for b, (p, j) in enumerate(blocks):
            thr = jnp.where(tid_s[p, j] == before(p, j), qs[b] + res[b][:, :128], 0.0)
            loc = res[b][:, 128:]
            if b > 0:
                both = mm3(thr, pre[b])
                thr, loc = both[:, :128], both[:, 128:] + loc
            thr_s[h, pl.ds(b * BLK, BLK), :] = jnp.concatenate([thr, loc], axis=1)
        return carry

    lax.fori_loop(0, HERE, local_out, 0)
    local[O].wait()
    far_weights.wait()
    pass_weights.start()

    states = []
    for h in range(HERE):
        for step in range(1, REACH + 1):
            @pl.when(chip >= step)
            def _():
                exchange(h, step).wait_recv()
        state = wrecv_s[h].astype(F32)
        for step in (3, 2, 1):
            state = mm3(recv_s[step - 1, h, :, 0:128].astype(F32), state) + recv_s[step - 1, h, :, 128:256].astype(F32)
        states.append(halves(state))

    def outputs(half):
        done = []
        for h in range(HERE):
            both = thr_s[h, rows_of(half), :]
            o = both[:, 128:] + joined(halves(both[:, :128]), states[h])
            o = o * lax.rsqrt(jnp.mean(o * o, axis=-1, keepdims=True) + norm_eps)
            g = gain[:, pl.ds(pl.multiple_of(core * 256 + h * 128, 128), 128)]
            done.append((o * g).astype(BF16))
        return jnp.concatenate(done, axis=1)

    far_rows = pl.ds(pl.multiple_of(lax.rem(head + 2, nhead) * 64, 64), 64)
    hid_s[...] = outputs(other)
    swap_hid = remote(hid_s, hid2_s.at[core], hsem.at[0], hsem.at[1], at(0, other))
    swap_hid.start()
    far_other = remote(hid_s.at[far_rows], far_s.at[core], fsem.at[0], fsem.at[1], across(2))
    far_other.start()
    hid2_s[core] = outputs(core)
    far_same = remote(hid2_s.at[core, far_rows], far_s.at[core], fsem.at[2], fsem.at[3], along(2))
    far_same.start()
    swap_hid.wait()

    def term(step, cols):
        rows = pl.ds(pl.multiple_of(lax.rem(head + step + nhead, nhead) * 64, 64), 64)
        return dot(hid2_s[0, rows, :], wo_s[0:256, cols]) + dot(hid2_s[1, rows, :], wo_s[256:512, cols])

    parts = [slice(n * 512, (n + 1) * 512) for n in range(4)]

    def hop(d, n):
        return remote(rs_s.at[d, n], rr_s.at[d, n], rsend.at[d, n], rrecv.at[d, n], along(1 if d == 0 else -1))

    for n, cols in enumerate(parts):
        for d in range(2):
            rs_s[d, n] = term(1 if d == 0 else -1, cols).astype(BF16)
            hop(d, n).start()
    sums = [term(0, cols).astype(BF16).astype(F32) for cols in parts]
    pass_weights.wait()
    far_other.wait()
    far_same.wait()
    far = [far_s[0], far_s[1]]
    for n, cols in enumerate(parts):
        extra = dot(far[0], wf_s[0:256, cols]) + dot(far[1], wf_s[256:512, cols])
        sums[n] = sums[n] + extra.astype(BF16).astype(F32)
    for n, cols in enumerate(parts):
        for d in range(2):
            hop(d, n).wait()
            sums[n] = sums[n] + rr_s[d, n].astype(F32)
        out[:, cols] = sums[n].astype(BF16)
    for step in range(1, REACH + 1):
        @pl.when(chip + step < chips)
        def _():
            for h in range(HERE):
                exchange(h, step).wait_send()

    @pl.when(chip + 1 < chips)
    def _():
        next_same.wait_send()
        next_other.wait_send()


def body(tokens, turn_ids, q_weight, k_weight, v_weight, beta_weight, beta_bias, norm_gain, out_weight):
    any_ = pl.BlockSpec(memory_space=pl.ANY)
    vmem = pl.BlockSpec(memory_space=pltpu.VMEM)
    V = pltpu.VMEM
    D = tokens.shape[1]
    return pl.pallas_call(
        kernel,
        out_shape=jax.ShapeDtypeStruct((64, 2048), BF16),
        in_specs=[any_] * 6 + [vmem, vmem, any_],
        out_specs=vmem,
        scratch_shapes=[
            V((512, D), BF16), V((2, D, 256), BF16), V((2, D, 256), BF16), V((D, 256), BF16), V((8, D), BF16),
            V((512, D), BF16), V((2, 2, 128), jnp.int32), V((2, 2, 128), jnp.int32),
            V((2, 512, 256), F32), V((2, 512, 256), F32), V((512, 256), F32), V((512, 8), F32),
            V((2, 2, 128, 128), F32), V((2, 2, 128, 256), F32), V((2, 2, 256, 256), F32), V((2, 2, 16, 256), F32), V((128, 2048), BF16),
            V((16, 8, 128), F32), V((128, 2048), F32), V((16, 8, 128), F32),
            V((2, 2, 2, 2, 256, 256), BF16), V((2, 2, 2, 2, 128, 256), BF16), V((2, 2, 2, 128, 256), F32),
            V((2, 2, 128, 256), F32), V((2, 512, 256), F32),
            V((2, 128, 256), BF16), V((3, 2, 128, 256), BF16), V((2, 128, 128), BF16),
            V((256, 256), BF16), V((2, 256, 256), BF16),
            V((2, 64, 256), BF16), V((512, D), BF16), V((2, 4, 64, 512), BF16), V((2, 4, 64, 512), BF16),
            *[
                pltpu.SemaphoreType.DMA(shape)
                for shape in ((9,), (2,), (6,), (4, 2), (4, 2), (2,), (4,), (4,), (2, 4), (2, 4))
            ],
        ],
        compiler_params=pltpu.CompilerParams(
            collective_id=0, has_side_effects=True, vmem_limit_bytes=56 * 1024 * 1024
        ),
        cost_estimate=pl.CostEstimate(flops=5_000_000_000, bytes_accessed=14_000_000, transcendentals=10_000),
    )(
        tokens, turn_ids.reshape(2, 128), q_weight, k_weight, v_weight, beta_weight.T,
        beta_bias.reshape(1, 8), norm_gain.reshape(1, 512), out_weight,
    )


def solution(mesh):
    return jax.shard_map(
        body,
        mesh=mesh,
        in_specs=(
            P("seq", None),
            P("seq"),
            P(None, "head"),
            P(None, "head"),
            P(None, "head"),
            P(None, "head"),
            P("head"),
            P("head"),
            P("head", None),
        ),
        out_specs=P(("seq", "head"), None),
        check_vma=False,
    )
```

```python
import functools

import jax
import jax.numpy as jnp
from jax import lax
from jax.experimental import pallas as pl
from jax.experimental.pallas import tpu as pltpu
from jax.sharding import PartitionSpec as P

F32, BF16 = jnp.float32, jnp.bfloat16
MESH = pl.DeviceIdType.MESH
DK = 128
BLK = 128
REFL = 2 * BLK
NB = 4
HERE = 2
PARTS = [pl.ds(n * 512, 512) for n in range(4)]
FETCHED = PARTS
REACH = 4
key_eps = 1e-06
norm_eps = 1e-05

NN = (((1,), (0,)), ((), ()))
NT = (((1,), (1,)), ((), ()))


def dot(a, b, dims=NN):
    return lax.dot_general(a, b, dims, preferred_element_type=F32)


def halves(a):
    hi = a.astype(BF16)
    return hi, (a - hi.astype(F32)).astype(BF16)


def joined(a, b):
    (ah, al), (bh, bl) = a, b
    return dot(jnp.concatenate([ah, al, ah], axis=1), jnp.concatenate([bh, bh, bl], axis=0))


def mm3(a, b):
    return joined(halves(a), halves(b))


def iota(shape, axis):
    return lax.broadcasted_iota(jnp.int32, shape, axis)


def interleave(a, b):
    groups, lanes = a.shape[0] // 8, a.shape[1]
    return jnp.concatenate(
        [a.reshape(groups, 1, 8, lanes), b.reshape(groups, 1, 8, lanes)], axis=1
    ).reshape(groups * 16, lanes)


def token_of(r):
    return ((r >> 4) << 3) + (r & 7)


def time_of(r):
    return token_of(r) * 2 + ((r >> 3) & 1)


def normalize(v):
    return v * lax.rsqrt(jnp.sum(v * v, axis=-1, keepdims=True) + key_eps)


def kernel(
    tok, ids, qw, kw, vw, bw, bb, gain, ow,
    out,
    x_s, wk_s, wv_s, wq_s, bw_s, wo_s, ids_s, prev_s,
    k_s, v_s, q_s, beta_s, tid_s, vis_s, mask_s, end_s, spread_s,
    cs_s, bc_s, xs_s, u_s, kt_s, lw_s, duo_s, thr_s, loc_s,
    send_s, recv_s, wrecv_s, hid_s, hid2_s, far_s, wf_s, rs_s, rr_s,
    lsem, tsem, isem, esend, erecv, hsem, fsem, wsem, rsend, rrecv,
):
    seq = lax.axis_index("seq")
    head = lax.axis_index("head")
    nseq = lax.axis_size("seq")
    nhead = lax.axis_size("head")
    chips = nseq // 2
    chip, core = seq // 2, lax.rem(seq, 2)
    other = 1 - core

    def at(step, which):
        return (lax.rem(chip + step + chips, chips) * 2 + which, head)

    def along(step):
        return (seq, lax.rem(head + step + nhead, nhead))

    def across(step):
        return (chip * 2 + other, lax.rem(head + step + nhead, nhead))

    own_rows = pl.ds(pl.multiple_of(core * 256, 256), 256)
    def weights(ref, width, h):
        return ref.at[:, pl.ds(pl.multiple_of(core * HERE * width + h * width, 256), 256)]

    X, K0, BW, V0, K1, V1, Q, O, IDS = range(9)
    pairs = [
        (tok, x_s.at[own_rows]), (weights(kw, 256, 0), wk_s.at[0]), (bw, bw_s), (weights(vw, 256, 0), wv_s.at[0]),
        (weights(kw, 256, 1), wk_s.at[1]), (weights(vw, 256, 1), wv_s.at[1]), (weights(qw, 128, 0), wq_s), (ow, wo_s),
        (ids, ids_s.at[core]),
    ]
    local = [pltpu.make_async_copy(src, dst, lsem.at[n]) for n, (src, dst) in enumerate(pairs)]
    for c in local:
        c.start()

    barrier = pltpu.get_barrier_semaphore()
    mutual = [at(0, other), along(1), along(-1), along(2), across(2)]
    for peer in mutual:
        pl.semaphore_signal(barrier, inc=1, device_id=peer, device_id_type=MESH)
    for step in range(1, REACH + 1):
        @pl.when(chip >= step)
        def _():
            pl.semaphore_signal(barrier, inc=1, device_id=at(-step, core), device_id_type=MESH)
            if step == 1:
                pl.semaphore_signal(barrier, inc=1, device_id=at(-step, other), device_id_type=MESH)
    greeted = len(mutual) + jnp.minimum(chips - 1 - chip, REACH) + jnp.minimum(chips - 1 - chip, 1)

    def remote(src, dst, ssem, rsem, peer):
        return pltpu.make_async_remote_copy(
            src_ref=src, dst_ref=dst, send_sem=ssem, recv_sem=rsem, device_id=peer, device_id_type=MESH
        )

    swap_ids = remote(ids, ids_s.at[core], isem.at[0], isem.at[1], at(0, other))
    swap_tok = remote(tok, x_s.at[own_rows], tsem.at[0], tsem.at[1], at(0, other))
    next_same = remote(ids, prev_s.at[core], isem.at[2], isem.at[3], at(1, core))
    half_rows = pl.ds(pl.multiple_of(core * 256, 256), 256)
    far_weights = [
        remote(ow.at[half_rows, cols], wf_s.at[half_rows, cols], wsem.at[0, n], wsem.at[1, n], along(2))
        for n, cols in enumerate(FETCHED)
    ]
    pass_weights = [
        remote(wf_s.at[half_rows, cols], wf_s.at[half_rows, cols], wsem.at[2, n], wsem.at[3, n], at(0, other))
        for n, cols in enumerate(FETCHED)
    ]
    next_other = remote(ids, prev_s.at[core], isem.at[4], isem.at[5], at(1, other))

    sr, sc = iota((128, 2048), 0), iota((128, 2048), 1)
    spread_s[...] = (((sr >> 4) == ((sc & 127) >> 4)) & ((sr & 15) == (sc >> 7))).astype(F32).astype(BF16)

    def rows_of(half):
        return pl.ds(pl.multiple_of(half * 256, 256), 256)

    def project(rows, h):
        x = x_s[rows, :]
        k_s[h, rows, :] = dot(x, wk_s[h])
        v_s[h, rows, :] = dot(x, wv_s[h])

    def strengths(rows):
        beta_s[rows, :] = 2.0 * jax.nn.sigmoid(dot(x_s[rows, :], bw_s[...], NT) + bb[...])

    r128, c128 = iota((128, 128), 0), iota((128, 128), 1)
    eye = (r128 == c128).astype(F32)
    rr_, cc_ = iota((REFL, REFL), 0), iota((REFL, REFL), 1)
    earlier = time_of(rr_) > time_of(cc_)
    seen = token_of(iota((BLK, REFL), 1)) <= iota((BLK, REFL), 0)
    lanes16 = iota((16, 128), 1) // 16
    unit8 = iota((8, 128), 1) % 16
    order = [j * 8 + t for t in range(8) for j in range(2)]

    def odd_rows(m, size):
        return jnp.concatenate([m[i * size:(i + 1) * size] for i in range(1, 128 // size, 2)], axis=0)

    def even_rows(m, size):
        return jnp.concatenate([m[i * size:(i + 1) * size] for i in range(0, 128 // size, 2)], axis=0)

    def merged(even, odd, size):
        return jnp.concatenate(
            [m[i * size:(i + 1) * size] for i in range(64 // size) for m in (even, odd)], axis=0
        )

    def turns(half):
        for j in range(2):
            row = ids_s[half, pl.ds(j, 1), :].astype(F32)
            tcol = jnp.transpose(jnp.broadcast_to(row, (BLK, BLK)))
            rcol = interleave(tcol, tcol)
            rrow = jnp.transpose(rcol)
            mask_s[half, j] = jnp.where(
                earlier & (jnp.concatenate([rcol, rcol], axis=1) == jnp.concatenate([rrow, rrow], axis=0)), 1.0, 0.0
            )
            end_s[half, j] = jnp.where(rrow[:16] == jnp.max(row, axis=1, keepdims=True), 1.0, 0.0)
            vis_s[half, j] = jnp.where(seen & (jnp.concatenate([tcol, tcol], axis=1) == rrow), 1.0, 0.0)
            tid_s[half, j] = tcol

    def maps(units, arrived=lambda: None):
        systems, rhs, kts = [], [], []
        for half, h, j in units:
            block = pl.ds(pl.multiple_of(half * 256 + j * BLK, BLK), BLK)
            betas = beta_s[block, :]
            lane = iota(betas.shape, 1)
            mine = [
                jnp.sum(jnp.where(lane == core * 4 + h * 2 + r, betas, 0.0), axis=1, keepdims=True) for r in range(2)
            ]
            k0 = normalize(k_s[h, block, 0:128])
            k1 = normalize(k_s[h, block, 128:256])
            keys = interleave(k0, k1)
            bkeys = interleave(mine[0] * k0, mine[1] * k1)
            bvals = interleave(mine[0] * v_s[h, block, 0:128], mine[1] * v_s[h, block, 128:256])
            kt = halves(jnp.transpose(keys))
            kt_s[half, h, j, 0] = kt[0]
            kt_s[half, h, j, 1] = kt[1]
            systems.append(joined(halves(bkeys), kt) * mask_s[half, j])
            rhs.append(jnp.concatenate([-bkeys, bvals], axis=1))
            ending = end_s[half, j][:1].astype(BF16)
            kts.append((kt[0] * ending, kt[1] * ending))
        tiles = [a[lo:lo + 128, lo:lo + 128] for a in systems for lo in (0, 128)]
        for n, a in enumerate(tiles):
            acc = jnp.where(lanes16 == 0, a[0:16], 0.0)
            for g in range(1, 8):
                acc = jnp.where(lanes16 == g, a[g * 16:(g + 1) * 16], acc)
            for slot in range(n, 8, len(tiles)):
                cs_s[:, slot, :] = acc
        hi, low = halves(cs_s[...].reshape(128, 128))
        bc_s[...] = dot(hi, spread_s[...]) + dot(low, spread_s[...])
        solved = {}
        for place, i in enumerate(order):
            x = jnp.where(unit8 == i, 1.0, 0.0)
            for j in order[:place]:
                x = x - bc_s[i * 8:(i + 1) * 8, j * 128:(j + 1) * 128] * solved[j]
            solved[i] = x
            xs_s[i] = x
        ts = [
            jnp.where(r128 // 16 == c128 // 16, jnp.concatenate([xs_s[:, n, :]] * 8, axis=0), 0.0)
            for n in range(len(tiles))
        ]
        for size in (16, 32, 64):
            ro = odd_rows(r128, size)
            pick = (ro // (2 * size) == c128[:64] // (2 * size)) & ((c128[:64] // size) % 2 == 0)
            split = [halves(t) for t in ts]
            lows = [
                joined(halves(jnp.where(pick, odd_rows(a, size), 0.0)), t) for a, t in zip(tiles, split)
            ]
            zero = jnp.zeros((64, 128), F32)
            news = [
                joined((odd_rows(t[0], size), odd_rows(t[1], size)), halves(merged(zero, low, size)))
                for t, low in zip(split, lows)
            ]
            ts = [merged(even_rows(t, size), odd_rows(t, size) - new, size) for t, new in zip(ts, news)]
        split = [halves(t) for t in ts]
        tops = [joined(split[2 * n], halves(rhs[n][:128])) for n in range(len(units))]
        mids = [
            rhs[n][128:] - joined(halves(systems[n][128:, :128]), halves(tops[n])) for n in range(len(units))
        ]
        lows = [joined(split[2 * n + 1], halves(mids[n])) for n in range(len(units))]
        lws = []
        for n, (half, h, j) in enumerate(units):
            u = halves(jnp.concatenate([tops[n], lows[n]], axis=0))
            u_s[half, h, j, 0] = u[0]
            u_s[half, h, j, 1] = u[1]
            lws.append(joined(kts[n], u))
        arrived()
        for n, (half, h, j) in enumerate(units):
            last = jnp.max(ids_s[half, pl.ds(j, 1), :].astype(F32), axis=1, keepdims=True)
            lift = jnp.where(before(half, j) == last, eye + lws[n][:, :128], 0.0)
            lws[n] = jnp.concatenate([lift, lws[n][:, 128:]], axis=1)
            lw_s[half, h, j] = lws[n]
        for n, (half, h, j) in enumerate(units):
            if j == 1:
                duo_s[half, h] = after(lws[n], lws[n - 1])

    def after(late, early):
        pair = mm3(late[:, :128], early)
        return jnp.concatenate([pair[:, :128], pair[:, 128:] + late[:, 128:]], axis=1)

    def before(half, j):
        if j == 1:
            return jnp.max(ids_s[half, pl.ds(0, 1), :].astype(F32), axis=1, keepdims=True)
        first = jnp.max(prev_s[1, pl.ds(1, 1), :].astype(F32), axis=1, keepdims=True)
        first = jnp.where(chip == 0, -1.0, first)
        inner = jnp.max(ids_s[0, pl.ds(1, 1), :].astype(F32), axis=1, keepdims=True)
        return jnp.where(half == 0, first, inner)

    def exchange(h, step):
        if step == REACH:
            return remote(
                send_s.at[h, :, pl.ds(128, 128)], wrecv_s.at[h], esend.at[step - 1, h], erecv.at[step - 1, h], at(step, core)
            )
        return remote(
            send_s.at[h], recv_s.at[step - 1, h], esend.at[step - 1, h], erecv.at[step - 1, h], at(step, core)
        )

    def send_maps(h):
        send_s[h] = after(duo_s[1, h], duo_s[0, h]).astype(BF16)
        for step in range(1, REACH + 1):
            @pl.when(chip + step < chips)
            def _():
                exchange(h, step).start()

    for n in (X, K0, V0):
        local[n].wait()
    project(rows_of(core), 0)
    for n in (K1, V1):
        local[n].wait()
    project(rows_of(core), 1)
    pl.semaphore_wait(barrier, greeted)
    for c in (swap_ids, swap_tok, *far_weights):
        c.start()

    @pl.when(chip + 1 < chips)
    def _():
        next_same.start()
        next_other.start()

    for step in range(1, REACH + 1):
        @pl.when(chip < step)
        def _():
            if step == REACH:
                wrecv_s[...] = jnp.zeros_like(wrecv_s)
            else:
                recv_s[step - 1] = jnp.zeros(recv_s.shape[1:], BF16)
            if step == 1:
                prev_s[...] = jnp.zeros_like(prev_s)

    for n in (BW, IDS):
        local[n].wait()
    strengths(rows_of(core))
    turns(core)

    def ids_arrived():
        swap_ids.wait()

        @pl.when(chip >= 1)
        def _():
            next_same.wait_recv()
            next_other.wait_recv()

    maps([(core, h, j) for h in range(HERE) for j in range(2)], ids_arrived)
    turns(other)
    swap_tok.wait()
    project(rows_of(other), 0)
    project(rows_of(other), 1)
    strengths(rows_of(other))
    maps([(other, h, j) for h in range(HERE) for j in range(2)])
    send_maps(0)
    send_maps(1)

    local[Q].wait()
    q_s[...] = dot(x_s[...], wq_s[...])

    def local_out(h, carry):
        second = duo_s[0, h]
        pre = (None, lw_s[0, h, 0], second, after(lw_s[1, h, 0], second))
        blocks = [(b // 2, b % 2) for b in range(NB)]
        qs = [
            normalize(q_s[pl.ds(b * BLK, BLK), pl.ds(pl.multiple_of(h * 128, 128), 128)]) for b in range(NB)
        ]
        scores = [
            joined(halves(qs[b]), (kt_s[p, h, j, 0], kt_s[p, h, j, 1])) * vis_s[p, j] for b, (p, j) in enumerate(blocks)
        ]
        res = [
            joined(halves(scores[b]), (u_s[p, h, j, 0], u_s[p, h, j, 1])) for b, (p, j) in enumerate(blocks)
        ]
        for b, (p, j) in enumerate(blocks):
            thr = jnp.where(tid_s[p, j] == before(p, j), qs[b] + res[b][:, :128], 0.0)
            loc = res[b][:, 128:]
            if b > 0:
                both = mm3(thr, pre[b])
                thr, loc = both[:, :128], both[:, 128:] + loc
            hi, low = halves(thr)
            thr_s[h, 0, pl.ds(b * BLK, BLK), :] = hi
            thr_s[h, 1, pl.ds(b * BLK, BLK), :] = low
            loc_s[h, pl.ds(b * BLK, BLK), :] = loc
        return carry

    lax.fori_loop(0, HERE, local_out, 0)
    local[O].wait()

    def share(n):
        far_weights[n].wait()
        pass_weights[n].start()

    for n in range(3):
        share(n)

    states = []
    for h in range(HERE):
        for step in range(1, REACH + 1):
            @pl.when(chip >= step)
            def _():
                exchange(h, step).wait_recv()
        state = wrecv_s[h].astype(F32)
        for step in (3, 2, 1):
            lift = recv_s[step - 1, h, :, 0:128]
            state = dot(
                jnp.concatenate([lift, lift], axis=1), jnp.concatenate(halves(state), axis=0)
            ) + recv_s[step - 1, h, :, 128:256].astype(F32)
        states.append(halves(state))

    def outputs(half):
        done = []
        for h in range(HERE):
            rows = rows_of(half)
            o = loc_s[h, rows, :] + joined((thr_s[h, 0, rows, :], thr_s[h, 1, rows, :]), states[h])
            o = o * lax.rsqrt(jnp.mean(o * o, axis=-1, keepdims=True) + norm_eps)
            g = gain[:, pl.ds(pl.multiple_of(core * 256 + h * 128, 128), 128)]
            done.append((o * g).astype(BF16))
        return jnp.concatenate(done, axis=1)

    far_rows = pl.ds(pl.multiple_of(lax.rem(head + 2, nhead) * 64, 64), 64)
    hid_s[...] = outputs(other)
    swap_hid = remote(hid_s, hid2_s.at[core], hsem.at[0], hsem.at[1], at(0, other))
    swap_hid.start()
    far_other = remote(hid_s.at[far_rows], far_s.at[core], fsem.at[0], fsem.at[1], across(2))
    far_other.start()
    hid2_s[core] = outputs(core)
    far_same = remote(hid2_s.at[core, far_rows], far_s.at[core], fsem.at[2], fsem.at[3], along(2))
    far_same.start()
    swap_hid.wait()

    def term(step, cols):
        rows = pl.ds(pl.multiple_of(lax.rem(head + step + nhead, nhead) * 64, 64), 64)
        return dot(hid2_s[0, rows, :], wo_s[0:256, cols]) + dot(hid2_s[1, rows, :], wo_s[256:512, cols])

    def hop(d, n):
        return remote(rs_s.at[d, n], rr_s.at[d, n], rsend.at[d, n], rrecv.at[d, n], along(1 if d == 0 else -1))

    for n, cols in enumerate(PARTS):
        for d in range(2):
            rs_s[d, n] = term(1 if d == 0 else -1, cols).astype(BF16)
            hop(d, n).start()
    share(3)
    sums = [term(0, cols).astype(BF16).astype(F32) for cols in PARTS]
    for c in pass_weights:
        c.wait()
    far_other.wait()
    far_same.wait()
    far = [far_s[0], far_s[1]]
    for n, cols in enumerate(FETCHED):
        extra = dot(far[0], wf_s[0:256, cols]) + dot(far[1], wf_s[256:512, cols])
        sums[n] = sums[n] + extra.astype(BF16).astype(F32)
    for n, cols in enumerate(PARTS):
        for d in range(2):
            hop(d, n).wait()
            sums[n] = sums[n] + rr_s[d, n].astype(F32)
        out[:, cols] = sums[n].astype(BF16)
    for step in range(1, REACH + 1):
        @pl.when(chip + step < chips)
        def _():
            for h in range(HERE):
                exchange(h, step).wait_send()

    @pl.when(chip + 1 < chips)
    def _():
        next_same.wait_send()
        next_other.wait_send()


def body(tokens, turn_ids, q_weight, k_weight, v_weight, beta_weight, beta_bias, norm_gain, out_weight):
    any_ = pl.BlockSpec(memory_space=pl.ANY)
    vmem = pl.BlockSpec(memory_space=pltpu.VMEM)
    V = pltpu.VMEM
    D = tokens.shape[1]
    return pl.pallas_call(
        kernel,
        out_shape=jax.ShapeDtypeStruct((64, 2048), BF16),
        in_specs=[any_] * 6 + [vmem, vmem, any_],
        out_specs=vmem,
        scratch_shapes=[
            V((512, D), BF16), V((2, D, 256), BF16), V((2, D, 256), BF16), V((D, 256), BF16), V((8, D), BF16),
            V((512, D), BF16), V((2, 2, 128), jnp.int32), V((2, 2, 128), jnp.int32),
            V((2, 512, 256), F32), V((2, 512, 256), F32), V((512, 256), F32), V((512, 8), F32),
            V((2, 2, 128, 128), F32), V((2, 2, 128, 256), F32), V((2, 2, 256, 256), F32), V((2, 2, 16, 256), F32), V((128, 2048), BF16),
            V((16, 8, 128), F32), V((128, 2048), F32), V((16, 8, 128), F32),
            V((2, 2, 2, 2, 256, 256), BF16), V((2, 2, 2, 2, 128, 256), BF16), V((2, 2, 2, 128, 256), F32),
            V((2, 2, 128, 256), F32), V((2, 2, 512, 128), BF16), V((2, 512, 128), F32),
            V((2, 128, 256), BF16), V((3, 2, 128, 256), BF16), V((2, 128, 128), BF16),
            V((256, 256), BF16), V((2, 256, 256), BF16),
            V((2, 64, 256), BF16), V((512, D), BF16), V((2, 4, 64, 512), BF16), V((2, 4, 64, 512), BF16),
            *[
                pltpu.SemaphoreType.DMA(shape)
                for shape in ((9,), (2,), (6,), (4, 2), (4, 2), (2,), (4,), (4, 4), (2, 4), (2, 4))
            ],
        ],
        compiler_params=pltpu.CompilerParams(
            collective_id=0, has_side_effects=True, vmem_limit_bytes=56 * 1024 * 1024
        ),
        cost_estimate=pl.CostEstimate(flops=5_000_000_000, bytes_accessed=14_000_000, transcendentals=10_000),
    )(
        tokens, turn_ids.reshape(2, 128), q_weight, k_weight, v_weight, beta_weight.T,
        beta_bias.reshape(1, 8), norm_gain.reshape(1, 512), out_weight,
    )


def solution(mesh):
    return jax.shard_map(
        body,
        mesh=mesh,
        in_specs=(
            P("seq", None),
            P("seq"),
            P(None, "head"),
            P(None, "head"),
            P(None, "head"),
            P(None, "head"),
            P("head"),
            P("head"),
            P("head", None),
        ),
        out_specs=P(("seq", "head"), None),
        check_vma=False,
    )
```

```python
import functools

import jax
import jax.numpy as jnp
from jax import lax
from jax.experimental import pallas as pl
from jax.experimental.pallas import tpu as pltpu
from jax.sharding import PartitionSpec as P

F32, BF16 = jnp.float32, jnp.bfloat16
MESH = pl.DeviceIdType.MESH
DK = 128
BLK = 128
REFL = 2 * BLK
NB = 4
HERE = 2
PARTS = [pl.ds(n * 512, 512) for n in range(4)]
FETCHED = PARTS
REACH = 4
key_eps = 1e-06
norm_eps = 1e-05

NN = (((1,), (0,)), ((), ()))
NT = (((1,), (1,)), ((), ()))


def dot(a, b, dims=NN):
    return lax.dot_general(a, b, dims, preferred_element_type=F32)


def halves(a):
    hi = a.astype(BF16)
    return hi, (a - hi.astype(F32)).astype(BF16)


def joined(a, b):
    (ah, al), (bh, bl) = a, b
    return dot(jnp.concatenate([ah, al, ah], axis=1), jnp.concatenate([bh, bh, bl], axis=0))


def mm3(a, b):
    return joined(halves(a), halves(b))


def iota(shape, axis):
    return lax.broadcasted_iota(jnp.int32, shape, axis)


def interleave(a, b):
    groups, lanes = a.shape[0] // 8, a.shape[1]
    return jnp.concatenate(
        [a.reshape(groups, 1, 8, lanes), b.reshape(groups, 1, 8, lanes)], axis=1
    ).reshape(groups * 16, lanes)


def token_of(r):
    return ((r >> 4) << 3) + (r & 7)


def time_of(r):
    return token_of(r) * 2 + ((r >> 3) & 1)


def normalize(v):
    return v * lax.rsqrt(jnp.sum(v * v, axis=-1, keepdims=True) + key_eps)


def kernel(
    tok, ids, qw, kw, vw, bw, bb, gain, ow,
    out,
    x_s, wk_s, wv_s, wq_s, bw_s, wo_s, ids_s, prev_s,
    k_s, v_s, q_s, beta_s, tid_s, vis_s, mask_s, end_s, spread_s,
    cs_s, bc_s, xs_s, u_s, kt_s, lw_s, duo_s, thr_s, loc_s,
    send_s, recv_s, wrecv_s, hid_s, hid2_s, far_s, wf_s, rs_s, rr_s,
    lsem, tsem, isem, esend, erecv, hsem, fsem, wsem, rsend, rrecv,
):
    seq = lax.axis_index("seq")
    head = lax.axis_index("head")
    nseq = lax.axis_size("seq")
    nhead = lax.axis_size("head")
    chips = nseq // 2
    chip, core = seq // 2, lax.rem(seq, 2)
    other = 1 - core

    def at(step, which):
        return (lax.rem(chip + step + chips, chips) * 2 + which, head)

    def along(step):
        return (seq, lax.rem(head + step + nhead, nhead))

    def across(step):
        return (chip * 2 + other, lax.rem(head + step + nhead, nhead))

    own_rows = pl.ds(pl.multiple_of(core * 256, 256), 256)
    def weights(ref, width, h):
        return ref.at[:, pl.ds(pl.multiple_of(core * HERE * width + h * width, 256), 256)]

    X, K0, BW, V0, K1, V1, Q, O, IDS = range(9)
    pairs = [
        (tok, x_s.at[own_rows]), (weights(kw, 256, 0), wk_s.at[0]), (bw, bw_s), (weights(vw, 256, 0), wv_s.at[0]),
        (weights(kw, 256, 1), wk_s.at[1]), (weights(vw, 256, 1), wv_s.at[1]), (weights(qw, 128, 0), wq_s), (ow, wo_s),
        (ids, ids_s.at[core]),
    ]
    local = [pltpu.make_async_copy(src, dst, lsem.at[n]) for n, (src, dst) in enumerate(pairs)]
    for c in local:
        c.start()

    barrier = pltpu.get_barrier_semaphore()
    mutual = [at(0, other), along(1), along(-1), along(2), across(2)]
    for peer in mutual:
        pl.semaphore_signal(barrier, inc=1, device_id=peer, device_id_type=MESH)
    for step in range(1, REACH + 1):
        @pl.when(chip >= step)
        def _():
            pl.semaphore_signal(barrier, inc=1, device_id=at(-step, core), device_id_type=MESH)
            if step == 1:
                pl.semaphore_signal(barrier, inc=1, device_id=at(-step, other), device_id_type=MESH)
    @pl.when(lax.rem(chip, 2) == 0)
    def _():
        pl.semaphore_signal(barrier, inc=1, device_id=at(1, core), device_id_type=MESH)

    greeted = len(mutual) + lax.rem(chip, 2) + jnp.minimum(chips - 1 - chip, REACH) + jnp.minimum(chips - 1 - chip, 1)

    def remote(src, dst, ssem, rsem, peer):
        return pltpu.make_async_remote_copy(
            src_ref=src, dst_ref=dst, send_sem=ssem, recv_sem=rsem, device_id=peer, device_id_type=MESH
        )

    swap_ids = remote(ids, ids_s.at[core], isem.at[0], isem.at[1], at(0, other))
    swap_tok = remote(tok, x_s.at[own_rows], tsem.at[0], tsem.at[1], at(0, other))
    next_same = remote(ids, prev_s.at[core], isem.at[2], isem.at[3], at(1, core))
    half_rows = pl.ds(pl.multiple_of(core * 256, 256), 256)
    far_weights = [
        remote(ow.at[half_rows, cols], wf_s.at[half_rows, cols], wsem.at[0, n], wsem.at[1, n], along(2))
        for n, cols in enumerate(FETCHED[:3])
    ]
    odd = lax.rem(chip, 2)
    quarter = pl.ds(pl.multiple_of(core * 256 + odd * 128, 128), 128)
    far_weights.append(
        remote(ow.at[quarter, PARTS[3]], wf_s.at[quarter, PARTS[3]], wsem.at[0, 3], wsem.at[1, 3], along(2))
    )
    swap_weights = remote(
        wf_s.at[quarter, PARTS[3]], wf_s.at[quarter, PARTS[3]], wsem.at[4, 0], wsem.at[5, 0], at(1 - 2 * odd, core)
    )
    pass_weights = [
        remote(wf_s.at[half_rows, cols], wf_s.at[half_rows, cols], wsem.at[2, n], wsem.at[3, n], at(0, other))
        for n, cols in enumerate(FETCHED)
    ]
    next_other = remote(ids, prev_s.at[core], isem.at[4], isem.at[5], at(1, other))

    sr, sc = iota((128, 2048), 0), iota((128, 2048), 1)
    spread_s[...] = (((sr >> 4) == ((sc & 127) >> 4)) & ((sr & 15) == (sc >> 7))).astype(F32).astype(BF16)

    def rows_of(half):
        return pl.ds(pl.multiple_of(half * 256, 256), 256)

    def project(rows, h):
        x = x_s[rows, :]
        k_s[h, rows, :] = dot(x, wk_s[h])
        v_s[h, rows, :] = dot(x, wv_s[h])

    def strengths(rows):
        beta_s[rows, :] = 2.0 * jax.nn.sigmoid(dot(x_s[rows, :], bw_s[...], NT) + bb[...])

    r128, c128 = iota((128, 128), 0), iota((128, 128), 1)
    eye = (r128 == c128).astype(F32)
    rr_, cc_ = iota((REFL, REFL), 0), iota((REFL, REFL), 1)
    earlier = time_of(rr_) > time_of(cc_)
    seen = token_of(iota((BLK, REFL), 1)) <= iota((BLK, REFL), 0)
    lanes16 = iota((16, 128), 1) // 16
    unit8 = iota((8, 128), 1) % 16
    order = [j * 8 + t for t in range(8) for j in range(2)]

    def odd_rows(m, size):
        return jnp.concatenate([m[i * size:(i + 1) * size] for i in range(1, 128 // size, 2)], axis=0)

    def even_rows(m, size):
        return jnp.concatenate([m[i * size:(i + 1) * size] for i in range(0, 128 // size, 2)], axis=0)

    def merged(even, odd, size):
        return jnp.concatenate(
            [m[i * size:(i + 1) * size] for i in range(64 // size) for m in (even, odd)], axis=0
        )

    def turns(half):
        for j in range(2):
            row = ids_s[half, pl.ds(j, 1), :].astype(F32)
            tcol = jnp.transpose(jnp.broadcast_to(row, (BLK, BLK)))
            rcol = interleave(tcol, tcol)
            rrow = jnp.transpose(rcol)
            mask_s[half, j] = jnp.where(
                earlier & (jnp.concatenate([rcol, rcol], axis=1) == jnp.concatenate([rrow, rrow], axis=0)), 1.0, 0.0
            )
            end_s[half, j] = jnp.where(rrow[:16] == jnp.max(row, axis=1, keepdims=True), 1.0, 0.0)
            vis_s[half, j] = jnp.where(seen & (jnp.concatenate([tcol, tcol], axis=1) == rrow), 1.0, 0.0)
            tid_s[half, j] = tcol

    def maps(units, arrived=lambda: None):
        systems, rhs, kts = [], [], []
        for half, h, j in units:
            block = pl.ds(pl.multiple_of(half * 256 + j * BLK, BLK), BLK)
            betas = beta_s[block, :]
            lane = iota(betas.shape, 1)
            mine = [
                jnp.sum(jnp.where(lane == core * 4 + h * 2 + r, betas, 0.0), axis=1, keepdims=True) for r in range(2)
            ]
            k0 = normalize(k_s[h, block, 0:128])
            k1 = normalize(k_s[h, block, 128:256])
            keys = interleave(k0, k1)
            bkeys = interleave(mine[0] * k0, mine[1] * k1)
            bvals = interleave(mine[0] * v_s[h, block, 0:128], mine[1] * v_s[h, block, 128:256])
            kt = halves(jnp.transpose(keys))
            kt_s[half, h, j, 0] = kt[0]
            kt_s[half, h, j, 1] = kt[1]
            systems.append(joined(halves(bkeys), kt) * mask_s[half, j])
            rhs.append(jnp.concatenate([-bkeys, bvals], axis=1))
            ending = end_s[half, j][:1].astype(BF16)
            kts.append((kt[0] * ending, kt[1] * ending))
        tiles = [a[lo:lo + 128, lo:lo + 128] for a in systems for lo in (0, 128)]
        for n, a in enumerate(tiles):
            acc = jnp.where(lanes16 == 0, a[0:16], 0.0)
            for g in range(1, 8):
                acc = jnp.where(lanes16 == g, a[g * 16:(g + 1) * 16], acc)
            for slot in range(n, 8, len(tiles)):
                cs_s[:, slot, :] = acc
        hi, low = halves(cs_s[...].reshape(128, 128))
        bc_s[...] = dot(hi, spread_s[...]) + dot(low, spread_s[...])
        solved = {}
        for place, i in enumerate(order):
            x = jnp.where(unit8 == i, 1.0, 0.0)
            for j in order[:place]:
                x = x - bc_s[i * 8:(i + 1) * 8, j * 128:(j + 1) * 128] * solved[j]
            solved[i] = x
            xs_s[i] = x
        ts = [
            jnp.where(r128 // 16 == c128 // 16, jnp.concatenate([xs_s[:, n, :]] * 8, axis=0), 0.0)
            for n in range(len(tiles))
        ]
        for size in (16, 32, 64):
            ro = odd_rows(r128, size)
            pick = (ro // (2 * size) == c128[:64] // (2 * size)) & ((c128[:64] // size) % 2 == 0)
            split = [halves(t) for t in ts]
            lows = [
                joined(halves(jnp.where(pick, odd_rows(a, size), 0.0)), t) for a, t in zip(tiles, split)
            ]
            zero = jnp.zeros((64, 128), F32)
            news = [
                joined((odd_rows(t[0], size), odd_rows(t[1], size)), halves(merged(zero, low, size)))
                for t, low in zip(split, lows)
            ]
            ts = [merged(even_rows(t, size), odd_rows(t, size) - new, size) for t, new in zip(ts, news)]
        split = [halves(t) for t in ts]
        tops = [joined(split[2 * n], halves(rhs[n][:128])) for n in range(len(units))]
        mids = [
            rhs[n][128:] - joined(halves(systems[n][128:, :128]), halves(tops[n])) for n in range(len(units))
        ]
        lows = [joined(split[2 * n + 1], halves(mids[n])) for n in range(len(units))]
        lws = []
        for n, (half, h, j) in enumerate(units):
            u = halves(jnp.concatenate([tops[n], lows[n]], axis=0))
            u_s[half, h, j, 0] = u[0]
            u_s[half, h, j, 1] = u[1]
            lws.append(joined(kts[n], u))
        arrived()
        for n, (half, h, j) in enumerate(units):
            last = jnp.max(ids_s[half, pl.ds(j, 1), :].astype(F32), axis=1, keepdims=True)
            lift = jnp.where(before(half, j) == last, eye + lws[n][:, :128], 0.0)
            lws[n] = jnp.concatenate([lift, lws[n][:, 128:]], axis=1)
            lw_s[half, h, j] = lws[n]
        for n, (half, h, j) in enumerate(units):
            if j == 1:
                duo_s[half, h] = after(lws[n], lws[n - 1])

    def after(late, early):
        pair = mm3(late[:, :128], early)
        return jnp.concatenate([pair[:, :128], pair[:, 128:] + late[:, 128:]], axis=1)

    def before(half, j):
        if j == 1:
            return jnp.max(ids_s[half, pl.ds(0, 1), :].astype(F32), axis=1, keepdims=True)
        first = jnp.max(prev_s[1, pl.ds(1, 1), :].astype(F32), axis=1, keepdims=True)
        first = jnp.where(chip == 0, -1.0, first)
        inner = jnp.max(ids_s[0, pl.ds(1, 1), :].astype(F32), axis=1, keepdims=True)
        return jnp.where(half == 0, first, inner)

    def exchange(h, step):
        if step == REACH:
            return remote(
                send_s.at[h, :, pl.ds(128, 128)], wrecv_s.at[h], esend.at[step - 1, h], erecv.at[step - 1, h], at(step, core)
            )
        return remote(
            send_s.at[h], recv_s.at[step - 1, h], esend.at[step - 1, h], erecv.at[step - 1, h], at(step, core)
        )

    def send_maps(h):
        send_s[h] = after(duo_s[1, h], duo_s[0, h]).astype(BF16)
        for step in range(1, REACH + 1):
            @pl.when(chip + step < chips)
            def _():
                exchange(h, step).start()

    for n in (X, K0, V0):
        local[n].wait()
    project(rows_of(core), 0)
    for n in (K1, V1):
        local[n].wait()
    project(rows_of(core), 1)
    pl.semaphore_wait(barrier, greeted)
    for c in (swap_ids, swap_tok, far_weights[3], *far_weights[:3]):
        c.start()

    @pl.when(chip + 1 < chips)
    def _():
        next_same.start()
        next_other.start()

    for step in range(1, REACH + 1):
        @pl.when(chip < step)
        def _():
            if step == REACH:
                wrecv_s[...] = jnp.zeros_like(wrecv_s)
            else:
                recv_s[step - 1] = jnp.zeros(recv_s.shape[1:], BF16)
            if step == 1:
                prev_s[...] = jnp.zeros_like(prev_s)

    for n in (BW, IDS):
        local[n].wait()
    strengths(rows_of(core))
    turns(core)

    def ids_arrived():
        swap_ids.wait()

        @pl.when(chip >= 1)
        def _():
            next_same.wait_recv()
            next_other.wait_recv()

    maps([(core, h, j) for h in range(HERE) for j in range(2)], ids_arrived)
    turns(other)
    swap_tok.wait()
    project(rows_of(other), 0)
    project(rows_of(other), 1)
    far_weights[3].wait()
    swap_weights.start()
    strengths(rows_of(other))
    maps([(other, h, j) for h in range(HERE) for j in range(2)])
    send_maps(0)
    send_maps(1)

    local[Q].wait()
    q_s[...] = dot(x_s[...], wq_s[...])

    def local_out(h, carry):
        second = duo_s[0, h]
        pre = (None, lw_s[0, h, 0], second, after(lw_s[1, h, 0], second))
        blocks = [(b // 2, b % 2) for b in range(NB)]
        qs = [
            normalize(q_s[pl.ds(b * BLK, BLK), pl.ds(pl.multiple_of(h * 128, 128), 128)]) for b in range(NB)
        ]
        scores = [
            joined(halves(qs[b]), (kt_s[p, h, j, 0], kt_s[p, h, j, 1])) * vis_s[p, j] for b, (p, j) in enumerate(blocks)
        ]
        res = [
            joined(halves(scores[b]), (u_s[p, h, j, 0], u_s[p, h, j, 1])) for b, (p, j) in enumerate(blocks)
        ]
        for b, (p, j) in enumerate(blocks):
            thr = jnp.where(tid_s[p, j] == before(p, j), qs[b] + res[b][:, :128], 0.0)
            loc = res[b][:, 128:]
            if b > 0:
                both = mm3(thr, pre[b])
                thr, loc = both[:, :128], both[:, 128:] + loc
            hi, low = halves(thr)
            thr_s[h, 0, pl.ds(b * BLK, BLK), :] = hi
            thr_s[h, 1, pl.ds(b * BLK, BLK), :] = low
            loc_s[h, pl.ds(b * BLK, BLK), :] = loc
        return carry

    lax.fori_loop(0, HERE, local_out, 0)
    local[O].wait()

    def share(n):
        far_weights[n].wait()
        pass_weights[n].start()

    swap_weights.wait()
    pass_weights[3].start()
    for n in range(2):
        share(n)

    states = []
    for h in range(HERE):
        for step in range(1, REACH + 1):
            @pl.when(chip >= step)
            def _():
                exchange(h, step).wait_recv()
        state = wrecv_s[h].astype(F32)
        for step in (3, 2, 1):
            lift = recv_s[step - 1, h, :, 0:128]
            state = dot(
                jnp.concatenate([lift, lift], axis=1), jnp.concatenate(halves(state), axis=0)
            ) + recv_s[step - 1, h, :, 128:256].astype(F32)
        states.append(halves(state))

    def outputs(half):
        done = []
        for h in range(HERE):
            rows = rows_of(half)
            o = loc_s[h, rows, :] + joined((thr_s[h, 0, rows, :], thr_s[h, 1, rows, :]), states[h])
            o = o * lax.rsqrt(jnp.mean(o * o, axis=-1, keepdims=True) + norm_eps)
            g = gain[:, pl.ds(pl.multiple_of(core * 256 + h * 128, 128), 128)]
            done.append((o * g).astype(BF16))
        return jnp.concatenate(done, axis=1)

    far_rows = pl.ds(pl.multiple_of(lax.rem(head + 2, nhead) * 64, 64), 64)
    hid_s[...] = outputs(other)
    swap_hid = remote(hid_s, hid2_s.at[core], hsem.at[0], hsem.at[1], at(0, other))
    swap_hid.start()
    far_other = remote(hid_s.at[far_rows], far_s.at[core], fsem.at[0], fsem.at[1], across(2))
    far_other.start()
    hid2_s[core] = outputs(core)
    far_same = remote(hid2_s.at[core, far_rows], far_s.at[core], fsem.at[2], fsem.at[3], along(2))
    far_same.start()
    swap_hid.wait()

    def term(step, cols):
        rows = pl.ds(pl.multiple_of(lax.rem(head + step + nhead, nhead) * 64, 64), 64)
        return dot(hid2_s[0, rows, :], wo_s[0:256, cols]) + dot(hid2_s[1, rows, :], wo_s[256:512, cols])

    def hop(d, n):
        return remote(rs_s.at[d, n], rr_s.at[d, n], rsend.at[d, n], rrecv.at[d, n], along(1 if d == 0 else -1))

    for n, cols in enumerate(PARTS):
        for d in range(2):
            rs_s[d, n] = term(1 if d == 0 else -1, cols).astype(BF16)
            hop(d, n).start()
    share(2)
    sums = [term(0, cols).astype(BF16).astype(F32) for cols in PARTS]
    for c in pass_weights:
        c.wait()
    far_other.wait()
    far_same.wait()
    far = [far_s[0], far_s[1]]
    for n, cols in enumerate(FETCHED):
        extra = dot(far[0], wf_s[0:256, cols]) + dot(far[1], wf_s[256:512, cols])
        sums[n] = sums[n] + extra.astype(BF16).astype(F32)
    for n, cols in enumerate(PARTS):
        for d in range(2):
            hop(d, n).wait()
            sums[n] = sums[n] + rr_s[d, n].astype(F32)
        out[:, cols] = sums[n].astype(BF16)
    for step in range(1, REACH + 1):
        @pl.when(chip + step < chips)
        def _():
            for h in range(HERE):
                exchange(h, step).wait_send()

    @pl.when(chip + 1 < chips)
    def _():
        next_same.wait_send()
        next_other.wait_send()


def body(tokens, turn_ids, q_weight, k_weight, v_weight, beta_weight, beta_bias, norm_gain, out_weight):
    any_ = pl.BlockSpec(memory_space=pl.ANY)
    vmem = pl.BlockSpec(memory_space=pltpu.VMEM)
    V = pltpu.VMEM
    D = tokens.shape[1]
    return pl.pallas_call(
        kernel,
        out_shape=jax.ShapeDtypeStruct((64, 2048), BF16),
        in_specs=[any_] * 6 + [vmem, vmem, any_],
        out_specs=vmem,
        scratch_shapes=[
            V((512, D), BF16), V((2, D, 256), BF16), V((2, D, 256), BF16), V((D, 256), BF16), V((8, D), BF16),
            V((512, D), BF16), V((2, 2, 128), jnp.int32), V((2, 2, 128), jnp.int32),
            V((2, 512, 256), F32), V((2, 512, 256), F32), V((512, 256), F32), V((512, 8), F32),
            V((2, 2, 128, 128), F32), V((2, 2, 128, 256), F32), V((2, 2, 256, 256), F32), V((2, 2, 16, 256), F32), V((128, 2048), BF16),
            V((16, 8, 128), F32), V((128, 2048), F32), V((16, 8, 128), F32),
            V((2, 2, 2, 2, 256, 256), BF16), V((2, 2, 2, 2, 128, 256), BF16), V((2, 2, 2, 128, 256), F32),
            V((2, 2, 128, 256), F32), V((2, 2, 512, 128), BF16), V((2, 512, 128), F32),
            V((2, 128, 256), BF16), V((3, 2, 128, 256), BF16), V((2, 128, 128), BF16),
            V((256, 256), BF16), V((2, 256, 256), BF16),
            V((2, 64, 256), BF16), V((512, D), BF16), V((2, 4, 64, 512), BF16), V((2, 4, 64, 512), BF16),
            *[
                pltpu.SemaphoreType.DMA(shape)
                for shape in ((9,), (2,), (6,), (4, 2), (4, 2), (2,), (4,), (6, 4), (2, 4), (2, 4))
            ],
        ],
        compiler_params=pltpu.CompilerParams(
            collective_id=0, has_side_effects=True, vmem_limit_bytes=56 * 1024 * 1024
        ),
        cost_estimate=pl.CostEstimate(flops=5_000_000_000, bytes_accessed=14_000_000, transcendentals=10_000),
    )(
        tokens, turn_ids.reshape(2, 128), q_weight, k_weight, v_weight, beta_weight.T,
        beta_bias.reshape(1, 8), norm_gain.reshape(1, 512), out_weight,
    )


def solution(mesh):
    return jax.shard_map(
        body,
        mesh=mesh,
        in_specs=(
            P("seq", None),
            P("seq"),
            P(None, "head"),
            P(None, "head"),
            P(None, "head"),
            P(None, "head"),
            P("head"),
            P("head"),
            P("head", None),
        ),
        out_specs=P(("seq", "head"), None),
        check_vma=False,
    )
```
